256 devices in a mesh: gz: 64 (over x, z, core), gy: 4 (over y).
Axes of the slice: x: 4, y: 4, z: 8, core: 2. Of those that a mesh axis runs over, the one named last changes fastest.
Arguments:
- velocity: float32 [3, 128, 8, 128], P(None, 'gz', 'gy'), may hold values from -6 to 6
- slip: float32 [3, 131072], P(None, ('gz', 'gy')), may hold values from -6 to 6
- rate: float32 [131072], P(('gz', 'gy')), may hold values from 0.5 to 4
- owner: int32 [131072, 1], P(('gz', 'gy')), may hold values from 0 to 63; in each aligned block of 512 rows (0 to 511, 512 to 1023, ...) at most 16 rows name the same one
- cell: int32 [131072], P(('gz', 'gy')), may hold values from 0 to 511
- count: int32 [256], P(('gz', 'gy')), may hold values from 256 to 512
- w_in: bfloat16 [12, 1024], replicated, may hold values from -1.75 to 1.75
- b_in: float32 [1024], replicated, may hold values from -3 to 3
- w_mid: bfloat16 [1024, 1024], replicated, may hold values from -0.1875 to 0.1875
- b_mid: float32 [1024], replicated, may hold values from -3 to 3
- w_out: bfloat16 [1024, 6], replicated, may hold values from -0.1875 to 0.1875
- tau_bar: bfloat16 [6, 128, 8, 128], P(None, 'gz', 'gy'), may hold values from -1.5 to 1.5
Outputs:
- stress: float32 [6, 128, 8, 128], P(None, 'gz', 'gy')
- velocity_bar: float32 [3, 128, 8, 128], P(None, 'gz', 'gy')
- slip_bar: float32 [3, 131072], P(None, ('gz', 'gy'))
- rate_bar: float32 [131072], P(('gz', 'gy'))
- grad_w_in: float32 [12, 1024], replicated
- grad_b_in: float32 [1024], replicated
- grad_w_mid: float32 [1024, 1024], replicated
- grad_b_mid: float32 [1024], replicated
- grad_w_out: float32 [1024, 6], replicated
The draws below stay inside these ranges and needn't reach their ends.
Inputs may be any that keep to these rules, and one draw needn't show every extreme that they name: Each particle's cell lies in the slab owner names, in the y-range of the particle's own device index along gy. Among the 512 slots of one device, at most 16 name the same slab, and that many do for some slab. The cell is flattened in the order z, y, x of the owner's block. The first count slots of a device are live, the others empty.
All inputs are finite; a program needn't handle non-finite values.
Results may differ from the reference program's by a relative error of at most 0.007.
Values sent between devices are 32-bit elements; how exact they have to be, the bound alone decides.
A program may use at most 64 MiB of HBM per device.

```python
import math
import jax
import jax.numpy as jnp
import numpy as np
from jax import lax

CZ = 2
CY = 2
NX = 128
H = 1024
F_IN = 12
N_OUT = 6
P_DEV = 512
CAP = 16
CELLS_DEV = 512
NZ = 128
NY = 8
PARTS_SIZE = 131072
N_GZ = 64
N_GY = 4


def place_ends(values, rng, low, largest):
    extent = values.shape
    spot = [jax.random.randint(jax.random.fold_in(rng, axis), (), 0, extent[axis]) for axis in range(len(extent))]
    values = values.at[tuple(spot)].set(low)
    longest = extent.index(max(extent))
    spot[longest] = (spot[longest] + 1) % extent[longest]
    return values.at[tuple(spot)].set(largest)


def block_levels(rng, shape, split, smallest, high):
    def one(position, parts):
        steps = jax.random.uniform(jax.random.fold_in(jax.random.fold_in(rng, 6), position), (parts,), jnp.float32, smallest / len(split), high / len(split))
        return jnp.repeat(jnp.exp(steps), shape[position] // parts).reshape((-1,) + (1,) * (len(shape) - position - 1))

    gain = one(*split[0])
    for cut in split[1:]:
        gain = gain * one(*cut)
    return gain


def cumulative_ranks(amount, slope):
    loads = [(1 << 20) // math.isqrt(standing ** slope) + 1 for standing in range(1, amount + 1)]
    width = 1 + sum(loads) // (1 << 30)
    return np.cumsum(np.array([max(1, weight // width) for weight in loads]))


def skewed_ids(key, extent, amount, lean):
    grid = cumulative_ranks(amount, lean)
    ticket = jax.random.randint(jax.random.fold_in(key, 1), extent, 0, int(grid[amount - 1]))
    standing = jnp.searchsorted(jnp.asarray(grid, jnp.int32), ticket, side="right")
    return jax.random.permutation(jax.random.fold_in(key, 2), amount)[standing].astype(jnp.int32)


def shared_out(stream_key, own, number, rows, number_of, top, limit, slope):
    sequence = jax.random.permutation(stream_key, number_of)
    crowded, usual = shares(number_of, rows * top, limit, slope, True), shares(number_of, rows * top, limit, slope, False)
    places = jnp.arange(number_of)

    def named(sizes, offset_by):
        used = int((sizes > 0).sum())
        fixed = max(1, used // 4)
        passed = fixed + (places - fixed + offset_by * (used - fixed)) % max(1, number_of - fixed)
        return jnp.zeros((number_of,), jnp.int32).at[sequence[jnp.where(places < fixed, places, passed)]].set(jnp.asarray(sizes, jnp.int32))

    sizes = jnp.where(number % 4 == 0, named(crowded, number // 4), named(usual, number - number // 4 - 1))
    mixed = jax.random.permutation(jax.random.fold_in(own, 3), number_of)
    donor, sink = mixed[0:number_of // 2 * 2:2], mixed[1:number_of // 2 * 2:2]
    room = jnp.minimum(sizes[donor] - 1, limit - sizes[sink]) // 2
    room = jnp.where((donor == sequence[0]) | (sink == sequence[0]) | (sizes[sink] == 0), 0, jnp.maximum(room, 0))
    passed = jax.random.randint(jax.random.fold_in(own, 4), (number_of // 2,), 0, 1 << 20) % (room + 1)
    sizes = sizes.at[donor].add(-passed).at[sink].add(passed)
    members = jnp.searchsorted(jnp.cumsum(sizes), jnp.arange(rows * top), side="right").astype(jnp.int32)
    listing = members.reshape(top, rows).T
    listing = listing[jax.random.permutation(jax.random.fold_in(own, 1), rows)]
    offset_by = jax.random.randint(jax.random.fold_in(own, 2), (rows, 1), 0, top)
    return jnp.take_along_axis(listing, (jnp.arange(top)[None, :] + offset_by) % top, axis=1)


def shares(number_of, total, most, lean, full):
    weights = [(1 << 20) // math.isqrt(standing ** lean) + 1 for standing in range(1, number_of + 1)]
    largest = most if full else min(most, max(-(-total // number_of), total * weights[0] // sum(weights)))
    least = 1 if total - largest >= number_of - 1 else 0
    given, rest = [largest] + [least] * (number_of - 1), total - largest - least * (number_of - 1)
    while rest > 0:
        movable = [i for i in range(1, number_of) if given[i] < largest] or [i for i in range(1, number_of) if given[i] < most]
        pool, remaining = sum([weights[i] for i in movable]), rest
        for i in movable:
            extra = min(most - given[i], max(1, remaining * weights[i] // pool), rest)
            given[i] = given[i] + extra
            rest = rest - extra
    return np.array(given)


def gaussian(key, shape, spread, reach, split=(), held_as=jnp.bfloat16):
    gain = block_levels(key, shape, split, -0.22, 0.18) if split else 1.0
    values = jax.random.normal(key, shape, jnp.float32) * spread * gain
    return jnp.minimum(jnp.maximum(values, -reach), reach).astype(held_as)


def setup_inputs(seed: int = 0) -> dict:
    arg_keys = jax.random.split(jax.random.key(seed), 13)
    velocity = gaussian(arg_keys[0], (3, NZ, NY, NX), 1.0, 6.0, ((1, 64), (2, 4)), jnp.float32)
    slip = gaussian(arg_keys[1], (3, PARTS_SIZE), 1.0, 6.0, ((1, 256),), jnp.float32)
    rate = jnp.clip(jnp.exp(math.log(4.0) - 2.0794415 * jax.random.uniform(arg_keys[2], (PARTS_SIZE,), jnp.float32) ** block_levels(arg_keys[2], (PARTS_SIZE,), ((0, 256),), -0.2, 0.2)), 0.5, 4.0)
    owner_keys = jax.random.split(jax.random.fold_in(arg_keys[3], 1), PARTS_SIZE // P_DEV)
    owner_turns = jax.random.permutation(jax.random.fold_in(arg_keys[3], 3), PARTS_SIZE // P_DEV)
    owner = jax.vmap(lambda own, number: shared_out(jax.random.fold_in(arg_keys[3], 2), own, number, P_DEV, N_GZ, 1, CAP, 2))(owner_keys, owner_turns).reshape((PARTS_SIZE, 1))
    cell = place_ends(skewed_ids(arg_keys[4], (PARTS_SIZE,), CELLS_DEV, 1), jax.random.fold_in(arg_keys[4], 3), 0, CELLS_DEV - 1).astype(jnp.int32)
    count = place_ends(jax.random.randint(arg_keys[5], (N_GZ * N_GY,), P_DEV // 2, P_DEV + 1), jax.random.fold_in(arg_keys[5], 1), P_DEV // 2, P_DEV).astype(jnp.int32)
    w_in = gaussian(arg_keys[6], (F_IN, H), F_IN ** -0.5, 1.75)
    b_in = gaussian(arg_keys[7], (H,), 0.5, 3.0, (), jnp.float32)
    w_mid = gaussian(arg_keys[8], (H, H), H ** -0.5, 0.1875)
    b_mid = gaussian(arg_keys[9], (H,), 0.5, 3.0, (), jnp.float32)
    w_out = gaussian(arg_keys[10], (H, N_OUT), H ** -0.5, 0.1875)
    tau_bar = gaussian(arg_keys[11], (N_OUT, NZ, NY, NX), 0.25, 1.5, ((1, 64), (2, 4)))
    return {"velocity": velocity, "slip": slip, "rate": rate, "owner": owner, "cell": cell, "count": count, "w_in": w_in, "b_in": b_in, "w_mid": w_mid, "b_mid": b_mid, "w_out": w_out, "tau_bar": tau_bar}


def derive(field, axis):
    return (jnp.roll(field, -1, axis) - jnp.roll(field, 1, axis)) * 0.5


def dsilu(value):
    sig = jax.nn.sigmoid(value)
    return sig * (1.0 + value * (1.0 - sig))


def reference(velocity, slip, rate, owner, cell, count, w_in, b_in, w_mid, b_mid, w_out, tau_bar):
    slots = jnp.arange(PARTS_SIZE, dtype=jnp.int32)
    device = slots // P_DEV
    live = (slots % P_DEV) < count[device]
    ycol = device % N_GY
    zpos = owner[:, 0] * CZ + cell // (CY * NX)
    ypos = ycol * CY + (cell // NX) % CY
    xpos = cell % NX
    global_id = ((zpos * NY + ypos) * NX + xpos).astype(jnp.int32)
    force = jnp.where(live[None, :], rate[None, :] * slip, 0.0)
    source = jax.ops.segment_sum(force.T, global_id, NZ * NY * NX).T.reshape(3, NZ, NY, NX)
    grads = jnp.stack([derive(velocity[i], a) for i in range(3) for a in range(3)])
    feats = jnp.concatenate([grads, source], 0).astype(jnp.bfloat16)
    plane_feats = feats.transpose(1, 0, 2, 3).reshape(NZ, F_IN, NY * NX)
    plane_bar = tau_bar.transpose(1, 0, 2, 3).reshape(NZ, N_OUT, NY * NX)
    win = w_in.astype(jnp.float32)
    wmid = w_mid.astype(jnp.float32)
    wout = w_out.astype(jnp.float32)

    def plane(carry, inputs):
        gin, gbin, gmid, gbmid, gout = carry
        fts, tb = inputs
        ftf = fts.astype(jnp.float32)
        tbf = tb.astype(jnp.float32)
        pre1 = jnp.einsum('fh,fc->hc', win, ftf) + b_in[:, None]
        h1 = jax.nn.silu(pre1).astype(jnp.bfloat16)
        h1f = h1.astype(jnp.float32)
        pre2 = jnp.einsum('gh,gc->hc', wmid, h1f) + b_mid[:, None]
        h2 = jax.nn.silu(pre2).astype(jnp.bfloat16)
        h2f = h2.astype(jnp.float32)
        stress = jnp.einsum('ho,hc->oc', wout, h2f)
        gout = gout + jnp.einsum('hc,oc->ho', h2f, tbf)
        g2 = (jnp.einsum('ho,oc->hc', wout, tbf) * dsilu(pre2)).astype(jnp.bfloat16).astype(jnp.float32)
        gmid = gmid + jnp.einsum('gc,hc->gh', h1f, g2)
        gbmid = gbmid + jnp.sum(g2, 1)
        g1 = (jnp.einsum('gh,hc->gc', wmid, g2) * dsilu(pre1)).astype(jnp.bfloat16).astype(jnp.float32)
        gin = gin + jnp.einsum('fc,hc->fh', ftf, g1)
        gbin = gbin + jnp.sum(g1, 1)
        fbar = jnp.einsum('fh,hc->fc', win, g1)
        return (gin, gbin, gmid, gbmid, gout), (stress, fbar)

    init = (jnp.zeros((F_IN, H), jnp.float32), jnp.zeros((H,), jnp.float32),
            jnp.zeros((H, H), jnp.float32), jnp.zeros((H,), jnp.float32),
            jnp.zeros((H, N_OUT), jnp.float32))
    sums, planes = lax.scan(plane, init, (plane_feats, plane_bar))
    grad_w_in, grad_b_in, grad_w_mid, grad_b_mid, grad_w_out = sums
    stress = planes[0].reshape(NZ, N_OUT, NY, NX).transpose(1, 0, 2, 3)
    feats_bar = planes[1].reshape(NZ, F_IN, NY, NX).transpose(1, 0, 2, 3)
    velocity_bar = jnp.stack([-(derive(feats_bar[3 * i], 0) + derive(feats_bar[3 * i + 1], 1)
                                + derive(feats_bar[3 * i + 2], 2)) for i in range(3)])
    source_bar = feats_bar[9:12].reshape(3, NZ * NY * NX)
    back = source_bar[:, global_id]
    slip_bar = jnp.where(live[None, :], rate[None, :] * back, 0.0)
    rate_bar = jnp.where(live, jnp.sum(slip * back, 0), 0.0)
    return (stress, velocity_bar, slip_bar, rate_bar, grad_w_in, grad_b_in,
            grad_w_mid, grad_b_mid, grad_w_out)
```

```python
import jax
import jax.numpy as jnp
from jax import lax
from jax.experimental import pallas as pl
from jax.experimental.pallas import tpu as pltpu
from jax.sharding import PartitionSpec as P

F32, BF16, I32 = jnp.float32, jnp.bfloat16, jnp.int32
NX_, NZ_, NC_, NY_ = 4, 8, 2, 4
HID, CELLS, SLOTS, CAP = 1024, 512, 512, 16
BLK = 256
NBLK = HID // BLK

(
    G_P1,
    G_P2,
    G_H1,
    G_H2,
    G_RZ,
    G_RX,
    G_SC,
    G_S1,
    G_S2,
    G_S3,
    G_S5,
    G_S6,
    G_S7,
    G_BIG,
) = range(14)
B_CORE, B_R1, B_R2, B_RZ, B_GZ, B_G2, B_G1, B_FO, B_FR = (G_BIG + NBLK * i for i in range(9))
N_SEMS = G_BIG + NBLK * 9


def nn(a, b):
    return lax.dot_general(a, b, (((1,), (0,)), ((), ())), preferred_element_type=F32)


def nt(a, b):
    return lax.dot_general(a, b, (((1,), (1,)), ((), ())), preferred_element_type=F32)


def tn(a, b):
    return lax.dot_general(a, b, (((0,), (0,)), ((), ())), preferred_element_type=F32)


def three(value):
    high = value.astype(BF16).astype(F32)
    rest = value - high
    middle = rest.astype(BF16).astype(F32)
    return high, middle, rest - middle


def iota(shape, axis):
    return lax.broadcasted_iota(I32, shape, axis)


def body(
    pk,
    cnt,
    w_in,
    b_in,
    w_mid_any,
    b_mid,
    w_out,
    out,
    sm_out,
    po,
    w_mid,
    w_in16,
    w_out16,
    v4,
    hz,
    hy,
    feats,
    m_send,
    r1,
    t1,
    r2,
    onehot,
    fs,
    back2,
    h1,
    h1t,
    ds1,
    h2t,
    g2t,
    g1t,
    cs,
    cb,
    a1,
    b1,
    p2,
    b2,
    p3,
    b3,
    zz,
    y2,
    ssm,
    sc,
    sa,
    sb1,
    spt,
    sb2,
    sz,
    sy,
    sx,
    sxo,
    fb4,
    hz2,
    hy2,
    rts,
    u2,
    t2,
    bk,
    send,
    recv,
    local,
):
    gz, gy = lax.axis_index("gz"), lax.axis_index("gy")
    x, z, c, y = gz // 16, (gz // 2) % 8, gz % 2, gy
    xc = x * 2 + c

    def dev(px, py, pz, pc):
        return {
            "gz": (lax.rem(px, NX_) * NZ_ + lax.rem(pz, NZ_)) * NC_ + lax.rem(pc, NC_),
            "gy": lax.rem(py, NY_),
        }

    def line(gz_, gy_):
        return {"gz": lax.rem(gz_, NX_ * NZ_ * NC_), "gy": lax.rem(gy_, NY_)}

    def start(group, src, dst, where):
        pltpu.make_async_remote_copy(
            src_ref=src,
            dst_ref=dst,
            send_sem=send.at[group],
            recv_sem=recv.at[group],
            device_id=where,
            device_id_type=pl.DeviceIdType.MESH,
        ).start()

    def arrived(group, whole):
        pltpu.make_async_copy(whole, whole, recv.at[group]).wait()

    def left(group, whole):
        pltpu.make_async_copy(whole, whole, send.at[group]).wait()

    load_w = pltpu.make_async_copy(w_mid_any, w_mid, local.at[0])
    load_w.start()

    sibling = dev(x, y, z, c + 1)
    partners = [dev(x + k // 2, y, z, c + k % 2) for k in range(1, 8)]
    partners += [dev(x, y + k, z, c) for k in range(1, 4)]
    partners += [dev(x, y, z + k, c) for k in range(1, 8)]
    partners += [line(gz + 63 + 2 * c, gy)]
    barrier = pltpu.get_barrier_semaphore()
    for who in partners:
        pl.semaphore_signal(barrier, inc=1, device_id=who, device_id_type=pl.DeviceIdType.MESH)

    for k in range(4):
        v4[k] = pk[0:8, 128 * k : 128 * k + 128]
    lane = iota((1, SLOTS), 1)
    live = lane < cnt[0]
    owner = pk[14:15, :].astype(I32)
    row = (owner >> 4) * 16 + (owner & 1) * 8 + ((owner >> 1) & 7)
    member = jnp.where(iota((64, SLOTS), 0) == row, 1.0, 0.0)
    member16 = member.astype(BF16)
    earlier = jnp.where(iota((SLOTS, SLOTS), 0) < iota((SLOTS, SLOTS), 1), 1.0, 0.0).astype(BF16)
    place = jnp.sum(nn(member16, earlier) * member, axis=0, keepdims=True).astype(I32)
    force = jnp.where(live, pk[6:7, :] * pk[3:6, :], 0.0)
    four = jnp.concatenate([force, pk[7:8, :]], 0)
    sub = iota((128, SLOTS), 0)
    mine = (sub // 4) == place
    wide = jnp.where(mine, jnp.concatenate([four] * 32, 0), 0.0)
    packed = nt(member16, jnp.concatenate(three(wide), 0).astype(BF16))
    packed = packed[:, 0:128] + packed[:, 128:256] + packed[:, 256:384]
    m_send[...] = packed.reshape(8, 8, 128)

    pl.semaphore_wait(barrier, len(partners))

    for k in range(1, 8):
        px, pc = lax.rem(x + k // 2, NX_), lax.rem(c + k % 2, NC_)
        start(G_P1, m_send.at[px * 2 + pc], r1.at[xc], dev(px, y, z, pc))

    def halo(group, src, to_z, to_y):
        start(group, src.at[pl.ds(2, 2)], to_z.at[0], line(gz + 1, gy))
        start(group, src.at[pl.ds(0, 2)], to_z.at[1], line(gz + 63, gy))
        start(group, src.at[1], to_y.at[0, 0], line(gz, gy + 1))
        start(group, src.at[3], to_y.at[0, 1], line(gz, gy + 1))
        start(group, src.at[0], to_y.at[1, 0], line(gz, gy + 3))
        start(group, src.at[2], to_y.at[1, 1], line(gz, gy + 3))

    halo(G_H1, v4, hz, hy)

    w_in16[...] = jnp.zeros_like(w_in16)
    w_in16[0:12, :] = w_in[...].astype(F32)
    w_out16[...] = jnp.zeros_like(w_out16)
    w_out16[0:6, :] = w_out[...].astype(F32)
    tau = jnp.concatenate([pk[8:14, :], jnp.zeros((10, CELLS), F32)], 0)
    tau16 = tau.astype(BF16)
    tau_one = jnp.where(iota((16, CELLS), 0) == 6, 1.0, tau).astype(BF16)

    def back_two(q, carry):
        cols = pl.ds(pl.multiple_of(q * BLK, BLK), BLK)
        back2[:, cols] = tn(tau16, w_out16[:, cols].astype(BF16))
        return carry

    lax.fori_loop(0, NBLK, back_two, 0)

    r1[xc] = m_send[xc]
    arrived(G_P1, r1.at[pl.ds(0, 7)])
    for k in range(8):
        t1[k] = r1[:, k, :]
    for k in range(1, 8):
        pz = lax.rem(z + k, NZ_)
        start(G_P2, t1.at[pz], r2.at[z], dev(x, y, pz, c))
    r2[z] = t1[z]

    def difference(tiles, from_z, from_y, k):
        kz, ky = k // 2, k % 2
        dz = (tiles[2 + ky] - from_z[0, ky]) if kz == 0 else (from_z[1, ky] - tiles[ky])
        dy = (tiles[2 * kz + 1] - from_y[0, kz]) if ky == 0 else (from_y[1, kz] - tiles[2 * kz])
        return dz * 0.5, dy * 0.5

    def along_x(value):
        return (pltpu.roll(value, 127, 1) - pltpu.roll(value, 1, 1)) * 0.5

    arrived(G_H1, r1)
    feats[...] = jnp.where(iota((16, CELLS), 0) == 12, 1.0, 0.0)
    for k in range(4):
        dz, dy = difference(v4, hz, hy, k)
        for a, d in enumerate((dz, dy, along_x(v4[k]))):
            for i in range(3):
                feats[3 * i + a : 3 * i + a + 1, 128 * k : 128 * k + 128] = d[i : i + 1]

    arrived(G_P2, r2.at[pl.ds(0, 7)])
    got = r2[...].reshape(64, 128)
    cell_of = iota((64, CELLS), 1).astype(F32)
    group_of = iota((64, 128), 1) // 4
    parts = three(got)
    for s in range(CAP):
        rows = slice(64 * s, 64 * s + 64)
        onehot[rows, :] = jnp.where(got[:, 4 * s + 3 : 4 * s + 4] == cell_of, 1.0, 0.0).astype(BF16)
        for j, part in enumerate(parts):
            fs[rows, 128 * j : 128 * j + 128] = jnp.where(group_of == s, part, 0.0).astype(BF16)

    def fold(wide_):
        total = wide_[0:128] + wide_[128:256] + wide_[256:384]
        total = jnp.sum(total.reshape(16, 8, total.shape[1]), axis=0)
        return total[0:3] + total[4:7]

    feats[9:12, :] = fold(tn(fs[...], onehot[...]))
    load_w.wait()

    feats16 = feats[...].astype(BF16)

    def first(q, carry):
        cols = pl.ds(pl.multiple_of(q * BLK, BLK), BLK)
        pre = tn(feats16, w_in16[:, cols].astype(BF16)) + b_in[:, cols]
        sig = jax.nn.sigmoid(pre)
        hidden = pre * sig
        h1t[:, cols] = hidden.astype(BF16)
        ds1[:, cols] = sig * (1.0 + pre * (1.0 - sig))
        h1[cols, :] = hidden.T.astype(BF16)
        return carry

    lax.fori_loop(0, NBLK, first, 0)

    def me1(p):
        return x * (1 - p) + y * p

    def me2(p):
        return y * (1 - p) + x * p

    def peer1(p, k):
        return dev(x + k * (1 - p), y + k * p, z, c)

    def peer2(p, k):
        return dev(x + k * p, y + k * (1 - p), z, c)

    def s1(q):
        p = lax.rem(q, 2)
        arrived(B_CORE + q, cb.at[q])
        a1[q] = a1[q] + cb[q]
        for k in (2, 1, 3):
            to = lax.rem(me1(p) + k, 4)
            rows = pl.ds(pl.multiple_of(to * 128, 128), 128)
            start(B_R1 + q, a1.at[q, rows], b1.at[q, k - 1], peer1(p, k))

    half = HID // 2

    def second(q, carry):
        cols = pl.ds(pl.multiple_of(q * BLK, BLK), BLK)
        pre = nn(h1t[...], w_mid[:, cols]) + b_mid[:, cols]
        sig = jax.nn.sigmoid(pre)
        hidden = (pre * sig).astype(BF16)
        h2t[:, cols] = hidden
        delta = (back2[:, cols] * (sig * (1.0 + pre * (1.0 - sig)))).astype(BF16)
        g2t[:, cols] = delta
        cs[q] = nn(h1[pl.ds(pl.multiple_of((1 - c) * half, half), half), :], delta)
        start(B_CORE + q, cs.at[q], cb.at[q], sibling)
        a1[q] = nn(h1[pl.ds(pl.multiple_of(c * half, half), half), :], delta)
        by_hidden, by_delta = nn(tau_one, hidden), nn(tau_one, delta)
        ssm[16:32, cols] = jnp.where(iota((16, BLK), 0) == 6, by_delta, by_hidden)

        @pl.when(q > 0)
        def _():
            s1(q - 1)

        return carry

    lax.fori_loop(0, NBLK, second, 0)
    s1(NBLK - 1)

    def third(q, carry):
        cols = pl.ds(pl.multiple_of(q * BLK, BLK), BLK)
        delta = (nt(g2t[...], w_mid[cols, :]) * ds1[:, cols]).astype(BF16)
        g1t[:, cols] = delta
        ssm[0:16, cols] = nn(feats16, delta)
        return carry

    lax.fori_loop(0, NBLK, third, 0)
    start(G_SC, ssm.at[pl.ds(pl.multiple_of((1 - c) * 16, 16), 16)], sc, sibling)

    bar = nt(w_in16[...].astype(BF16), g1t[...])
    for k in range(4):
        fb4[k] = bar[0:8, 128 * k : 128 * k + 128]
    halo(G_H2, fb4, hz2, hy2)
    spread = jnp.concatenate([bar[9:12], jnp.zeros((1, CELLS), F32)], 0)
    spread = jnp.concatenate([spread] * 32, 0)
    picked = nt(onehot[...], jnp.concatenate(three(spread), 0).astype(BF16))
    back = jnp.zeros((64, 128), F32)
    for s in range(CAP):
        block = picked[64 * s : 64 * s + 64]
        block = block[:, 0:128] + block[:, 128:256] + block[:, 256:384]
        back = jnp.where(group_of == s, block, back)
    rts[...] = back.reshape(8, 8, 128)
    for k in range(1, 8):
        pz = lax.rem(z + k, NZ_)
        start(G_RZ, rts.at[pz], u2.at[z], dev(x, y, pz, c))
    u2[z] = rts[z]
    po[0:6, :] = nt(w_out16[...].astype(BF16), h2t[...])[0:6]

    def s2(q):
        p = q % 2
        arrived(B_R1 + q, b1.at[q])
        own = a1[q, pl.ds(pl.multiple_of(me1(p) * 128, 128), 128), :]
        p2[q] = own + b1[q, 0] + b1[q, 1] + b1[q, 2]
        for k in (2, 1, 3):
            to = lax.rem(me2(p) + k, 4)
            start(
                B_R2 + q, p2.at[q, pl.ds(pl.multiple_of(to * 32, 32), 32)], b2.at[q, k - 1], peer2(p, k)
            )

    def s3(q):
        p = q % 2
        arrived(B_R2 + q, b2.at[q])
        own = p2[q, pl.ds(pl.multiple_of(me2(p) * 32, 32), 32), :]
        total = own + b2[q, 0] + b2[q, 1] + b2[q, 2]
        for k in range(8):
            r, cc = k // 2, k % 2
            p3[q, k] = total[8 * r : 8 * r + 8, 128 * cc : 128 * cc + 128]
        for k in (4, 3, 5, 2, 6, 1, 7):
            pz = lax.rem(z + k, NZ_)
            start(B_RZ + q, p3.at[q, pz], b3.at[q, k - 1], dev(x, y, pz, c))

    def s4(q):
        arrived(B_RZ + q, b3.at[q])
        zz[q, z] = p3[q, z] + jnp.sum(b3[q], axis=0)
        for k in (4, 3, 5, 2, 6, 1, 7):
            start(B_GZ + q, zz.at[q, z], zz.at[q, z], dev(x, y, z + k, c))

    def s5(q):
        p = q % 2
        arrived(B_GZ + q, b3.at[q])
        own = pl.multiple_of(me2(p) * 32, 32)
        for k in range(8):
            r, cc = k // 2, k % 2
            y2[q, pl.ds(own + 8 * r, 8), 128 * cc : 128 * cc + 128] = zz[q, k]
        piece = y2.at[q, pl.ds(own, 32)]
        for k in (2, 1, 3):
            start(B_G2 + q, piece, piece, peer2(p, k))

    def region(q, core, d1):
        return out.at[pl.ds(pl.multiple_of(core * half + d1 * 128, 128), 128), BLK * q : BLK * q + BLK]

    def s6(q):
        p = q % 2
        arrived(B_G2 + q, b2.at[q])
        for k in (2, 1, 3):
            start(B_G1 + q, y2.at[q], region(q, c, me1(p)), peer1(p, k))
        start(B_FO + q, y2.at[q], region(q, c, me1(p)), sibling)
        out[pl.ds(pl.multiple_of(c * half + me1(p) * 128, 128), 128), BLK * q : BLK * q + BLK] = y2[q]

    def s7(q):
        p = q % 2
        arrived(B_G1 + q, b1.at[q])
        for k in (1, 2, 3):
            where = region(q, c, lax.rem(me1(p) + k, 4))
            start(B_FR + q, where, where, sibling)

    def s8(q):
        arrived(B_FO + q, p2.at[q])
        arrived(B_FR + q, b1.at[q])

    def m1():
        arrived(G_SC, sc)
        total = ssm[pl.ds(pl.multiple_of(c * 16, 16), 16), :] + sc[...]
        for k in range(4):
            sa[k] = total[:, 256 * k : 256 * k + 256]
        for k in (2, 1, 3):
            start(G_S1, sa.at[lax.rem(x + k, 4)], sb1.at[k - 1], dev(x + k, y, z, c))

    def m2():
        arrived(G_S1, sb1)
        total = sa[x] + sb1[0] + sb1[1] + sb1[2]
        for k in range(4):
            spt[k] = total[8 * (k // 2) : 8 * (k // 2) + 8, 128 * (k % 2) : 128 * (k % 2) + 128]
        for k in (2, 1, 3):
            start(G_S2, spt.at[lax.rem(y + k, 4)], sb2.at[k - 1], dev(x, y + k, z, c))

    def m3():
        arrived(G_S2, sb2)
        sz[z] = spt[y] + sb2[0] + sb2[1] + sb2[2]
        for k in (4, 3, 5, 2, 6, 1, 7):
            start(G_S3, sz.at[z], sz.at[z], dev(x, y, z + k, c))

    def m5():
        arrived(G_S3, b3.at[0])
        sy[y] = jnp.sum(sz[...], axis=0)
        for k in (2, 1, 3):
            start(G_S5, sy.at[y], sy.at[y], dev(x, y + k, z, c))

    def m6():
        arrived(G_S5, sb2)
        for k in range(4):
            sx[x, 8 * (k // 2) : 8 * (k // 2) + 8, 128 * (k % 2) : 128 * (k % 2) + 128] = sy[k]
        for k in (2, 1, 3):
            start(G_S6, sx.at[x], sx.at[x], dev(x + k, y, z, c))

    def m7():
        arrived(G_S6, sb1)
        start(G_S7, sx, sxo, sibling)

    def m8():
        arrived(G_S7, sc)
        for k in range(4):
            sm_out[pl.ds(pl.multiple_of(c * 16, 16), 16), 256 * k : 256 * k + 256] = sx[k]
            sm_out[pl.ds(pl.multiple_of((1 - c) * 16, 16), 16), 256 * k : 256 * k + 256] = sxo[k]

    def returned():
        arrived(G_RZ, u2.at[pl.ds(0, 7)])
        for k in range(8):
            t2[k] = u2[:, k, :]
        for k in range(1, 8):
            px, pc = lax.rem(x + k // 2, NX_), lax.rem(c + k % 2, NC_)
            start(G_RX, t2.at[px * 2 + pc], bk.at[xc], dev(px, y, z, pc))
        bk[xc] = t2[xc]

    def particles():
        arrived(G_RX, bk.at[pl.ds(0, 7)])
        rows = jnp.concatenate(three(bk[...].reshape(64, 128)), 1).astype(BF16)
        at = tn(rows, member16)
        at = jnp.where(jnp.concatenate([mine] * 3, 0), at, 0.0)
        at = fold(at)
        po[9:12, :] = jnp.where(live, pk[6:7, :] * at, 0.0)
        po[12:13, :] = jnp.where(live, jnp.sum(pk[3:6, :] * at, axis=0, keepdims=True), 0.0)

    def velocity_bar():
        arrived(G_H2, r1)
        for k in range(4):
            cols = slice(128 * k, 128 * k + 128)
            dz, dy = difference(fb4, hz2, hy2, k)
            dx = along_x(bar[:, cols])
            for i in range(3):
                total = dz[3 * i : 3 * i + 1] + dy[3 * i + 1 : 3 * i + 2] + dx[3 * i + 2 : 3 * i + 3]
                po[6 + i : 7 + i, cols] = -total

    s2(0)
    s2(1)
    m1()
    returned()
    velocity_bar()
    s3(0)
    s3(1)
    s2(2)
    s2(3)
    m2()
    particles()
    s4(0)
    s4(1)
    s3(2)
    s3(3)
    m3()
    s5(0)
    s5(1)
    s4(2)
    s4(3)
    m5()
    s6(0)
    s6(1)
    s5(2)
    s5(3)
    m6()
    s6(2)
    s6(3)
    m7()
    left(G_P1, r1.at[pl.ds(0, 7)])
    left(G_P2, r1.at[pl.ds(0, 7)])
    left(G_H1, r1)
    left(G_H2, r1)
    left(G_RZ, r1.at[pl.ds(0, 7)])
    left(G_RX, r1.at[pl.ds(0, 7)])
    left(G_SC, sc)
    left(G_S1, sb1)
    left(G_S2, sb2)
    left(G_S3, b3.at[0])
    left(G_S5, sb2)
    left(G_S6, sb1)
    for q in range(NBLK):
        left(B_CORE + q, cb.at[q])
        left(B_R1 + q, b1.at[q])
        left(B_R2 + q, b2.at[q])
        left(B_RZ + q, b3.at[q])
        left(B_GZ + q, b3.at[q])
        left(B_G2 + q, b2.at[q])
    s7(0)
    s7(1)
    m8()
    left(G_S7, sc)
    for q in range(2, NBLK):
        s7(q)
    for q in range(NBLK):
        s8(q)
        left(B_G1 + q, b1.at[q])
        left(B_FO + q, p2.at[q])
        left(B_FR + q, b1.at[q])


def finish(sm, po, stress, vbar, slip, rate, gin, gbin, gbmid, gout):
    for k in range(4):
        cols = slice(128 * k, 128 * k + 128)
        for i in range(6):
            stress[i, k // 2, k % 2 : k % 2 + 1, :] = po[i : i + 1, cols]
        for i in range(3):
            vbar[i, k // 2, k % 2 : k % 2 + 1, :] = po[6 + i : 7 + i, cols]
    slip[...] = po[9:12, :]
    rate[...] = po[12:13, :]
    gin[...] = sm[0:12, :]
    gbin[...] = sm[12:13, :]
    gbmid[...] = sm[22:23, :]
    gout[...] = sm[16:22, :]


def tiles(*shape, dtype=F32):
    return pltpu.VMEM(shape, dtype)


def shards(velocity, slip, rate, owner, cell, count, w_in, b_in, w_mid, b_mid, w_out, tau_bar):
    packed = jnp.concatenate(
        [
            velocity.reshape(3, CELLS),
            slip,
            rate.reshape(1, SLOTS),
            cell.astype(F32).reshape(1, SLOTS),
            tau_bar.astype(F32).reshape(6, CELLS),
            owner.astype(F32).reshape(1, SLOTS),
            jnp.zeros((1, CELLS), F32),
        ],
        0,
    )
    vmem = pl.BlockSpec(memory_space=pltpu.VMEM)
    big, sm, po = pl.pallas_call(
        body,
        name="adjoint",
        out_shape=(
            pltpu.VMEM((HID, HID), F32),
            pltpu.VMEM((32, HID), F32),
            pltpu.VMEM((16, CELLS), F32),
        ),
        in_specs=[
            vmem,
            pl.BlockSpec(memory_space=pltpu.SMEM),
            vmem,
            vmem,
            pl.BlockSpec(memory_space=pl.ANY),
            vmem,
            vmem,
        ],
        out_specs=(vmem, vmem, vmem),
        scratch_shapes=[
            tiles(HID, HID, dtype=BF16),
            tiles(16, HID),
            tiles(16, HID),
            tiles(4, 8, 128),
            tiles(2, 2, 8, 128),
            tiles(2, 2, 8, 128),
            tiles(16, CELLS),
            tiles(8, 8, 128),
            tiles(8, 8, 128),
            tiles(8, 8, 128),
            tiles(8, 8, 128),
            tiles(64 * CAP, CELLS, dtype=BF16),
            tiles(64 * CAP, 384, dtype=BF16),
            tiles(CELLS, HID),
            tiles(HID, CELLS, dtype=BF16),
            tiles(CELLS, HID, dtype=BF16),
            tiles(CELLS, HID),
            tiles(CELLS, HID, dtype=BF16),
            tiles(CELLS, HID, dtype=BF16),
            tiles(CELLS, HID, dtype=BF16),
            tiles(NBLK, HID // 2, BLK),
            tiles(NBLK, HID // 2, BLK),
            tiles(NBLK, HID // 2, BLK),
            tiles(NBLK, 3, 128, BLK),
            tiles(NBLK, 128, BLK),
            tiles(NBLK, 3, 32, BLK),
            tiles(NBLK, 8, 8, 128),
            tiles(NBLK, 7, 8, 128),
            tiles(NBLK, 8, 8, 128),
            tiles(NBLK, 128, BLK),
            tiles(32, HID),
            tiles(16, HID),
            tiles(4, 16, 256),
            tiles(3, 16, 256),
            tiles(4, 8, 128),
            tiles(3, 8, 128),
            tiles(8, 8, 128),
            tiles(4, 8, 128),
            tiles(4, 16, 256),
            tiles(4, 16, 256),
            tiles(4, 8, 128),
            tiles(2, 2, 8, 128),
            tiles(2, 2, 8, 128),
            tiles(8, 8, 128),
            tiles(8, 8, 128),
            tiles(8, 8, 128),
            tiles(8, 8, 128),
            pltpu.SemaphoreType.DMA((N_SEMS,)),
            pltpu.SemaphoreType.DMA((N_SEMS,)),
            pltpu.SemaphoreType.DMA((1,)),
        ],
        compiler_params=pltpu.CompilerParams(
            collective_id=0, has_side_effects=True, vmem_limit_bytes=48 << 20
        ),
    )(packed, count, w_in, b_in.reshape(1, HID), w_mid, b_mid.reshape(1, HID), w_out.T)
    out = [
        jax.ShapeDtypeStruct(s, F32)
        for s in (
            (6, 2, 2, 128),
            (3, 2, 2, 128),
            (3, SLOTS),
            (1, SLOTS),
            (12, HID),
            (1, HID),
            (1, HID),
            (6, HID),
        )
    ]
    stress, vbar, slip_bar, rate_bar, gin, gbin, gbmid, gout = pl.pallas_call(
        finish,
        name="finish",
        out_shape=out,
        in_specs=[vmem, vmem],
        out_specs=[vmem] * 8,
        compiler_params=pltpu.CompilerParams(vmem_limit_bytes=4 << 20),
    )(sm, po)
    return (
        stress,
        vbar,
        slip_bar,
        rate_bar.reshape(SLOTS),
        gin,
        gbin.reshape(HID),
        big,
        gbmid.reshape(HID),
        gout.T,
    )


def solution(mesh):
    return jax.shard_map(
        shards,
        mesh=mesh,
        in_specs=(
            P(None, "gz", "gy", None),
            P(None, ("gz", "gy")),
            P(("gz", "gy")),
            P(("gz", "gy"), None),
            P(("gz", "gy")),
            P(("gz", "gy")),
            P(),
            P(),
            P(),
            P(),
            P(),
            P(None, "gz", "gy", None),
        ),
        out_specs=(
            P(None, "gz", "gy", None),
            P(None, "gz", "gy", None),
            P(None, ("gz", "gy")),
            P(("gz", "gy")),
            P(),
            P(),
            P(),
            P(),
            P(),
        ),
        check_vma=False,
    )
```

```python
import jax
import jax.numpy as jnp
from jax import lax
from jax.experimental import pallas as pl
from jax.experimental.pallas import tpu as pltpu
from jax.sharding import PartitionSpec as P

F32, BF16, I32 = jnp.float32, jnp.bfloat16, jnp.int32
NX_, NZ_, NC_, NY_ = 4, 8, 2, 4
HID, CELLS, SLOTS, CAP = 1024, 512, 512, 16
BLK = 256
NBLK = HID // BLK

(
    G_P1,
    G_P2,
    G_H1,
    G_H2,
    G_RZ,
    G_RX,
    G_SC,
    G_S1,
    G_S2,
    G_S3,
    G_S5,
    G_S6,
    G_S7,
    G_BIG,
) = range(14)
B_CORE, B_RZ, B_GZ, B_FR = (G_BIG + NBLK * i for i in range(4))
B_R1, B_R2, B_G2, B_G1 = (G_BIG + NBLK * (4 + 2 * i) for i in range(4))
N_SEMS = G_BIG + NBLK * 12


def nn(a, b):
    return lax.dot_general(a, b, (((1,), (0,)), ((), ())), preferred_element_type=F32)


def nt(a, b):
    return lax.dot_general(a, b, (((1,), (1,)), ((), ())), preferred_element_type=F32)


def tn(a, b):
    return lax.dot_general(a, b, (((0,), (0,)), ((), ())), preferred_element_type=F32)


def three(value):
    high = value.astype(BF16).astype(F32)
    rest = value - high
    middle = rest.astype(BF16).astype(F32)
    return high, middle, rest - middle


def iota(shape, axis):
    return lax.broadcasted_iota(I32, shape, axis)


def body(
    velocity_in,
    slip_in,
    rate_in,
    owner_in,
    cell_in,
    cnt,
    w_in_in,
    b_in_in,
    w_mid_in,
    b_mid_in,
    w_out_in,
    tau_in,
    out,
    sm_out,
    po,
    velocity,
    slip,
    rate,
    owner,
    cell,
    w_in,
    b_in,
    b_mid,
    w_out,
    tau_bar,
    w_mid,
    w_in16,
    w_out16,
    tau_rows,
    v4,
    hz,
    hy,
    feats,
    m_send,
    r1,
    t1,
    r2,
    onehot,
    fs,
    back2,
    h1,
    h1t,
    ds1,
    h2t,
    g2t,
    g1t,
    cs,
    cb,
    a1,
    b1,
    p2,
    b2,
    p3,
    b3,
    zz,
    y2,
    ssm,
    sc,
    sa,
    sb1,
    spt,
    sb2,
    sz,
    sy,
    sx,
    sxo,
    fb4,
    hz2,
    hy2,
    rts,
    u2,
    t2,
    bk,
    send,
    recv,
    local,
):
    gz, gy = lax.axis_index("gz"), lax.axis_index("gy")
    x, z, c, y = gz // 16, (gz // 2) % 8, gz % 2, gy
    xc = x * 2 + c

    def dev(px, py, pz, pc):
        return {
            "gz": (lax.rem(px, NX_) * NZ_ + lax.rem(pz, NZ_)) * NC_ + lax.rem(pc, NC_),
            "gy": lax.rem(py, NY_),
        }

    def line(gz_, gy_):
        return {"gz": lax.rem(gz_, NX_ * NZ_ * NC_), "gy": lax.rem(gy_, NY_)}

    def start(group, src, dst, where):
        pltpu.make_async_remote_copy(
            src_ref=src,
            dst_ref=dst,
            send_sem=send.at[group],
            recv_sem=recv.at[group],
            device_id=where,
            device_id_type=pl.DeviceIdType.MESH,
        ).start()

    def arrived(group, whole):
        pltpu.make_async_copy(whole, whole, recv.at[group]).wait()

    def left(group, whole):
        pltpu.make_async_copy(whole, whole, send.at[group]).wait()

    sibling = dev(x, y, z, c + 1)
    partners = [dev(x + k // 2, y, z, c + k % 2) for k in range(1, 8)]
    partners += [dev(x, y + k, z, c) for k in range(1, 4)]
    partners += [dev(x, y, z + k, c) for k in range(1, 8)]
    partners += [line(gz + 63 + 2 * c, gy)]
    barrier = pltpu.get_barrier_semaphore()
    for who in partners:
        pl.semaphore_signal(barrier, inc=1, device_id=who, device_id_type=pl.DeviceIdType.MESH)

    loads = [
        pltpu.make_async_copy(src, dst, local.at[i])
        for i, (src, dst) in enumerate(
            (
                (owner_in, owner),
                (cell_in, cell),
                (rate_in, rate),
                (slip_in, slip),
                (velocity_in, velocity),
                (tau_in, tau_bar),
                (w_in_in, w_in),
                (w_out_in, w_out),
                (b_in_in, b_in),
                (b_mid_in, b_mid),
                (w_mid_in, w_mid),
            )
        )
    ]
    for load in loads:
        load.start()

    for load in loads[0:5]:
        load.wait()
    for k in range(4):
        for i in range(3):
            v4[k, i : i + 1, :] = velocity[i, k // 2, k % 2 : k % 2 + 1, :]
    lane = iota((1, SLOTS), 1)
    live = lane < cnt[0]
    slab = owner[...]
    row = (slab >> 4) * 16 + (slab & 1) * 8 + ((slab >> 1) & 7)
    member = jnp.where(iota((64, SLOTS), 0) == row, 1.0, 0.0)
    member16 = member.astype(BF16)
    earlier = jnp.where(iota((SLOTS, SLOTS), 0) < iota((SLOTS, SLOTS), 1), 1.0, 0.0).astype(BF16)
    place = jnp.sum(nn(member16, earlier) * member, axis=0, keepdims=True).astype(I32)
    force = jnp.where(live, rate[...] * slip[...], 0.0)
    four = jnp.concatenate([force, cell[...].astype(F32)], 0)
    sub = iota((128, SLOTS), 0)
    mine = (sub // 4) == place
    wide = jnp.where(mine, jnp.concatenate([four] * 32, 0), 0.0)
    packed = nt(member16, jnp.concatenate(three(wide), 0).astype(BF16))
    packed = packed[:, 0:128] + packed[:, 128:256] + packed[:, 256:384]
    m_send[...] = packed.reshape(8, 8, 128)

    pl.semaphore_wait(barrier, len(partners))

    for k in range(1, 8):
        px, pc = lax.rem(x + k // 2, NX_), lax.rem(c + k % 2, NC_)
        start(G_P1, m_send.at[px * 2 + pc], r1.at[xc], dev(px, y, z, pc))

    def halo(group, src, to_z, to_y):
        start(group, src.at[pl.ds(2, 2)], to_z.at[0], line(gz + 1, gy))
        start(group, src.at[pl.ds(0, 2)], to_z.at[1], line(gz + 63, gy))
        start(group, src.at[1], to_y.at[0, 0], line(gz, gy + 1))
        start(group, src.at[3], to_y.at[0, 1], line(gz, gy + 1))
        start(group, src.at[0], to_y.at[1, 0], line(gz, gy + 3))
        start(group, src.at[2], to_y.at[1, 1], line(gz, gy + 3))

    halo(G_H1, v4, hz, hy)

    for load in loads[5:10]:
        load.wait()
    w_in16[...] = jnp.zeros_like(w_in16)
    w_in16[0:12, :] = w_in[...].astype(F32)
    w_out16[...] = jnp.zeros_like(w_out16)
    w_out16[0:6, :] = w_out[...].astype(F32)
    tau_rows[...] = jnp.zeros_like(tau_rows)
    for i in range(6):
        for k in range(2):
            pair = tau_bar[i, k].astype(F32)
            for j in range(2):
                at = 256 * k + 128 * j
                tau_rows[i : i + 1, at : at + 128] = pair[j : j + 1]
    tau = tau_rows[...]
    tau16 = tau.astype(BF16)
    tau_one = jnp.where(iota((16, CELLS), 0) == 6, 1.0, tau).astype(BF16)

    def back_two(q, carry):
        cols = pl.ds(pl.multiple_of(q * BLK, BLK), BLK)
        back2[:, cols] = tn(tau16, w_out16[:, cols].astype(BF16))
        return carry

    lax.fori_loop(0, NBLK, back_two, 0)

    r1[xc] = m_send[xc]
    arrived(G_P1, r1.at[pl.ds(0, 7)])
    for k in range(8):
        t1[k] = r1[:, k, :]
    for k in range(1, 8):
        pz = lax.rem(z + k, NZ_)
        start(G_P2, t1.at[pz], r2.at[z], dev(x, y, pz, c))
    r2[z] = t1[z]

    def difference(tiles, from_z, from_y, k):
        kz, ky = k // 2, k % 2
        dz = (tiles[2 + ky] - from_z[0, ky]) if kz == 0 else (from_z[1, ky] - tiles[ky])
        dy = (tiles[2 * kz + 1] - from_y[0, kz]) if ky == 0 else (from_y[1, kz] - tiles[2 * kz])
        return dz * 0.5, dy * 0.5

    def along_x(value):
        return (pltpu.roll(value, 127, 1) - pltpu.roll(value, 1, 1)) * 0.5

    arrived(G_H1, r1)
    feats[...] = jnp.where(iota((16, CELLS), 0) == 12, 1.0, 0.0)
    for k in range(4):
        dz, dy = difference(v4, hz, hy, k)
        for a, d in enumerate((dz, dy, along_x(v4[k]))):
            for i in range(3):
                feats[3 * i + a : 3 * i + a + 1, 128 * k : 128 * k + 128] = d[i : i + 1]

    arrived(G_P2, r2.at[pl.ds(0, 7)])
    got = r2[...].reshape(64, 128)
    cell_of = iota((64, CELLS), 1).astype(F32)
    group_of = iota((64, 128), 1) // 4
    parts = three(got)
    for s in range(CAP):
        rows = slice(64 * s, 64 * s + 64)
        onehot[rows, :] = jnp.where(got[:, 4 * s + 3 : 4 * s + 4] == cell_of, 1.0, 0.0).astype(BF16)
        for j, part in enumerate(parts):
            fs[rows, 128 * j : 128 * j + 128] = jnp.where(group_of == s, part, 0.0).astype(BF16)

    def fold(wide_):
        total = wide_[0:128] + wide_[128:256] + wide_[256:384]
        total = jnp.sum(total.reshape(16, 8, total.shape[1]), axis=0)
        return total[0:3] + total[4:7]

    feats[9:12, :] = fold(tn(fs[...], onehot[...]))
    loads[10].wait()

    feats16 = feats[...].astype(BF16)

    def first(q, carry):
        cols = pl.ds(pl.multiple_of(q * BLK, BLK), BLK)
        pre = tn(feats16, w_in16[:, cols].astype(BF16)) + b_in[:, cols]
        sig = jax.nn.sigmoid(pre)
        hidden = pre * sig
        h1t[:, cols] = hidden.astype(BF16)
        ds1[:, cols] = sig * (1.0 + pre * (1.0 - sig))
        h1[cols, :] = hidden.T.astype(BF16)
        return carry

    lax.fori_loop(0, NBLK, first, 0)

    def me1(p):
        return x * (1 - p) + y * p

    def me2(p):
        return y * (1 - p) + x * p

    def peer1(p, k):
        return dev(x + k * (1 - p), y + k * p, z, c)

    def peer2(p, k):
        return dev(x + k * p, y + k * (1 - p), z, c)

    def s1(q):
        arrived(B_CORE + q, cb.at[q])
        for p in range(2):
            a1[q, p] = a1[q, p] + cb[q, :, 128 * p : 128 * p + 128]
            for k in (2, 1, 3):
                to = lax.rem(me1(p) + k, 4)
                rows = pl.ds(pl.multiple_of(to * 128, 128), 128)
                start(B_R1 + 2 * q + p, a1.at[q, p, rows], b1.at[q, p, k - 1], peer1(p, k))

    half = HID // 2

    def second(q, carry):
        cols = pl.ds(pl.multiple_of(q * BLK, BLK), BLK)
        pre = nn(h1t[...], w_mid[:, cols]) + b_mid[:, cols]
        sig = jax.nn.sigmoid(pre)
        hidden = (pre * sig).astype(BF16)
        h2t[:, cols] = hidden
        delta = (back2[:, cols] * (sig * (1.0 + pre * (1.0 - sig)))).astype(BF16)
        g2t[:, cols] = delta
        cs[q] = nn(h1[pl.ds(pl.multiple_of((1 - c) * half, half), half), :], delta)
        start(B_CORE + q, cs.at[q], cb.at[q], sibling)
        own = nn(h1[pl.ds(pl.multiple_of(c * half, half), half), :], delta)
        a1[q, 0] = own[:, 0:128]
        a1[q, 1] = own[:, 128:256]
        by_hidden, by_delta = nn(tau_one, hidden), nn(tau_one, delta)
        ssm[16:32, cols] = jnp.where(iota((16, BLK), 0) == 6, by_delta, by_hidden)

        @pl.when((q == 1) | (q == 2))
        def _():
            s1(q - 1)

        return carry

    lax.fori_loop(0, NBLK, second, 0)

    def s2(q):
        for p in range(2):
            arrived(B_R1 + 2 * q + p, b1.at[q, p])
            own = a1[q, p, pl.ds(pl.multiple_of(me1(p) * 128, 128), 128), :]
            p2[q, p] = own + b1[q, p, 0] + b1[q, p, 1] + b1[q, p, 2]
            for k in (2, 1, 3):
                rows = pl.ds(pl.multiple_of(lax.rem(me2(p) + k, 4) * 32, 32), 32)
                start(B_R2 + 2 * q + p, p2.at[q, p, rows], b2.at[q, p, k - 1], peer2(p, k))

    def s3(q):
        for p in range(2):
            arrived(B_R2 + 2 * q + p, b2.at[q, p])
            own = p2[q, p, pl.ds(pl.multiple_of(me2(p) * 32, 32), 32), :]
            total = own + b2[q, p, 0] + b2[q, p, 1] + b2[q, p, 2]
            for k in range(8):
                p3[q, k, 4 * p : 4 * p + 4, :] = total[4 * k : 4 * k + 4]
        for k in (4, 3, 5, 2, 6, 1, 7):
            pz = lax.rem(z + k, NZ_)
            start(B_RZ + q, p3.at[q, pz], b3.at[q, k - 1], dev(x, y, pz, c))

    def s4(q):
        arrived(B_RZ + q, b3.at[q])
        zz[q, z] = p3[q, z] + jnp.sum(b3[q], axis=0)
        for k in (4, 3, 5, 2, 6, 1, 7):
            start(B_GZ + q, zz.at[q, z], zz.at[q, z], dev(x, y, z + k, c))

    def s5(q):
        arrived(B_GZ + q, b3.at[q])
        for p in range(2):
            rows = pl.ds(pl.multiple_of(me2(p) * 32, 32), 32)
            y2[q, p, rows, :] = jnp.concatenate([zz[q, k, 4 * p : 4 * p + 4, :] for k in range(8)], 0)
            piece = y2.at[q, p, rows]
            for k in (2, 1, 3):
                start(B_G2 + 2 * q + p, piece, piece, peer2(p, k))

    def s6(q):
        for p in range(2):
            arrived(B_G2 + 2 * q + p, b2.at[q, p])
            rows = pl.ds(pl.multiple_of(c * half + me1(p) * 128, 128), 128)
            cols = slice(BLK * q + 128 * p, BLK * q + 128 * p + 128)
            for k in (2, 1, 3):
                start(B_G1 + 2 * q + p, y2.at[q, p], out.at[rows, cols], peer1(p, k))
            out[rows, cols] = y2[q, p]

    def s7(q):
        for p in range(2):
            arrived(B_G1 + 2 * q + p, b1.at[q, p])
        where = out.at[pl.ds(pl.multiple_of(c * half, half), half), BLK * q : BLK * q + BLK]
        start(B_FR + q, where, where, sibling)

    def s8(q):
        arrived(B_FR + q, cb.at[q])

    def m1():
        arrived(G_SC, sc)
        total = ssm[pl.ds(pl.multiple_of(c * 16, 16), 16), :] + sc[...]
        for k in range(4):
            sa[k] = total[:, 256 * k : 256 * k + 256]
        for k in (2, 1, 3):
            start(G_S1, sa.at[lax.rem(x + k, 4)], sb1.at[k - 1], dev(x + k, y, z, c))

    def m2():
        arrived(G_S1, sb1)
        total = sa[x] + sb1[0] + sb1[1] + sb1[2]
        for k in range(4):
            spt[k] = total[8 * (k // 2) : 8 * (k // 2) + 8, 128 * (k % 2) : 128 * (k % 2) + 128]
        for k in (2, 1, 3):
            start(G_S2, spt.at[lax.rem(y + k, 4)], sb2.at[k - 1], dev(x, y + k, z, c))

    def m3():
        arrived(G_S2, sb2)
        sz[z] = spt[y] + sb2[0] + sb2[1] + sb2[2]
        for k in (4, 3, 5, 2, 6, 1, 7):
            start(G_S3, sz.at[z], sz.at[z], dev(x, y, z + k, c))

    def m5():
        arrived(G_S3, b3.at[0])
        sy[y] = jnp.sum(sz[...], axis=0)
        for k in (2, 1, 3):
            start(G_S5, sy.at[y], sy.at[y], dev(x, y + k, z, c))

    def m6():
        arrived(G_S5, sb2)
        for k in range(4):
            sx[x, 8 * (k // 2) : 8 * (k // 2) + 8, 128 * (k % 2) : 128 * (k % 2) + 128] = sy[k]
        for k in (2, 1, 3):
            start(G_S6, sx.at[x], sx.at[x], dev(x + k, y, z, c))

    def m7():
        arrived(G_S6, sb1)
        start(G_S7, sx, sxo, sibling)

    def m8():
        arrived(G_S7, sc)
        for k in range(4):
            sm_out[pl.ds(pl.multiple_of(c * 16, 16), 16), 256 * k : 256 * k + 256] = sx[k]
            sm_out[pl.ds(pl.multiple_of((1 - c) * 16, 16), 16), 256 * k : 256 * k + 256] = sxo[k]

    def returned():
        arrived(G_RZ, u2.at[pl.ds(0, 7)])
        for k in range(8):
            t2[k] = u2[:, k, :]
        for k in range(1, 8):
            px, pc = lax.rem(x + k // 2, NX_), lax.rem(c + k % 2, NC_)
            start(G_RX, t2.at[px * 2 + pc], bk.at[xc], dev(px, y, z, pc))
        bk[xc] = t2[xc]

    def particles():
        arrived(G_RX, bk.at[pl.ds(0, 7)])
        rows = jnp.concatenate(three(bk[...].reshape(64, 128)), 1).astype(BF16)
        at = tn(rows, member16)
        at = jnp.where(jnp.concatenate([mine] * 3, 0), at, 0.0)
        at = fold(at)
        po[9:12, :] = jnp.where(live, rate[...] * at, 0.0)
        po[12:13, :] = jnp.where(live, jnp.sum(slip[...] * at, axis=0, keepdims=True), 0.0)

    def velocity_bar():
        arrived(G_H2, r1)
        for k in range(4):
            cols = slice(128 * k, 128 * k + 128)
            dz, dy = difference(fb4, hz2, hy2, k)
            dx = along_x(bar[:, cols])
            for i in range(3):
                total = dz[3 * i : 3 * i + 1] + dy[3 * i + 1 : 3 * i + 2] + dx[3 * i + 2 : 3 * i + 3]
                po[6 + i : 7 + i, cols] = -total

    def third(q, carry):
        cols = pl.ds(pl.multiple_of(q * BLK, BLK), BLK)
        delta = (nt(g2t[...], w_mid[cols, :]) * ds1[:, cols]).astype(BF16)
        g1t[:, cols] = delta
        ssm[0:16, cols] = nn(feats16, delta)
        return carry

    lax.fori_loop(0, NBLK, third, 0)
    start(G_SC, ssm.at[pl.ds(pl.multiple_of((1 - c) * 16, 16), 16)], sc, sibling)

    s2(0)
    s1(2)
    bar = nt(w_in16[...].astype(BF16), g1t[...])
    for k in range(4):
        fb4[k] = bar[0:8, 128 * k : 128 * k + 128]
    halo(G_H2, fb4, hz2, hy2)
    s2(1)
    s1(3)
    spread = jnp.concatenate([bar[9:12], jnp.zeros((1, CELLS), F32)], 0)
    spread = jnp.concatenate([spread] * 32, 0)
    picked = nt(onehot[...], jnp.concatenate(three(spread), 0).astype(BF16))
    back = jnp.zeros((64, 128), F32)
    for s in range(CAP):
        block = picked[64 * s : 64 * s + 64]
        block = block[:, 0:128] + block[:, 128:256] + block[:, 256:384]
        back = jnp.where(group_of == s, block, back)
    rts[...] = back.reshape(8, 8, 128)
    for k in range(1, 8):
        pz = lax.rem(z + k, NZ_)
        start(G_RZ, rts.at[pz], u2.at[z], dev(x, y, pz, c))
    u2[z] = rts[z]
    po[0:6, :] = nt(w_out16[...].astype(BF16), h2t[...])[0:6]

    s3(0)
    m1()
    returned()
    s2(2)
    s3(1)
    velocity_bar()
    s2(3)
    s4(0)
    s3(2)
    m2()
    s4(1)
    s3(3)
    particles()
    s5(0)
    m3()
    s4(2)
    s5(1)
    s6(0)
    s4(3)
    s6(1)
    s5(2)
    m5()
    s5(3)
    s6(2)
    m6()
    s6(3)
    s7(0)
    left(G_P1, r1.at[pl.ds(0, 7)])
    left(G_P2, r1.at[pl.ds(0, 7)])
    left(G_H1, r1)
    left(G_H2, r1)
    left(G_RZ, r1.at[pl.ds(0, 7)])
    left(G_RX, r1.at[pl.ds(0, 7)])
    left(G_SC, sc)
    left(G_S1, sb1)
    left(G_S2, sb2)
    left(G_S3, b3.at[0])
    left(G_S5, sb2)
    for q in range(NBLK):
        left(B_CORE + q, cb.at[q])
        left(B_RZ + q, b3.at[q])
        left(B_GZ + q, b3.at[q])
        for p in range(2):
            left(B_R1 + 2 * q + p, b1.at[q, p])
            left(B_R2 + 2 * q + p, b2.at[q, p])
            left(B_G2 + 2 * q + p, b2.at[q, p])
    s7(1)
    m7()
    s7(2)
    m8()
    left(G_S6, sb1)
    left(G_S7, sc)
    s7(3)
    for q in range(NBLK):
        for p in range(2):
            left(B_G1 + 2 * q + p, b1.at[q, p])
    for q in range(NBLK):
        s8(q)
        left(B_FR + q, cb.at[q])


def finish(big, sm, po, stress, vbar, slip, rate, gin, gbin, gmid, gbmid, gout, sem):
    copies = [
        pltpu.make_async_copy(big.at[pl.ds(128 * k, 128)], gmid.at[pl.ds(128 * k, 128)], sem.at[k])
        for k in range(8)
    ]
    for copy in copies:
        copy.start()
    for k in range(4):
        cols = slice(128 * k, 128 * k + 128)
        for i in range(6):
            stress[i, k // 2, k % 2 : k % 2 + 1, :] = po[i : i + 1, cols]
        for i in range(3):
            vbar[i, k // 2, k % 2 : k % 2 + 1, :] = po[6 + i : 7 + i, cols]
    slip[...] = po[9:12, :]
    rate[...] = po[12:13, :]
    gin[...] = sm[0:12, :]
    gbin[...] = sm[12:13, :]
    gbmid[...] = sm[22:23, :]
    gout[...] = sm[16:22, :]
    for copy in copies:
        copy.wait()


def tiles(*shape, dtype=F32):
    return pltpu.VMEM(shape, dtype)


def in_hbm(value):
    return pltpu.with_memory_space_constraint(value, pltpu.HBM)


def in_vmem(value):
    return pltpu.with_memory_space_constraint(value, pltpu.VMEM)


def shards(velocity, slip, rate, owner, cell, count, w_in, b_in, w_mid, b_mid, w_out, tau_bar):
    vmem = pl.BlockSpec(memory_space=pltpu.VMEM)
    hbm = pl.BlockSpec(memory_space=pltpu.HBM)
    big, sm, po = pl.pallas_call(
        body,
        name="adjoint",
        out_shape=(
            pltpu.VMEM((HID, HID), F32),
            pltpu.VMEM((32, HID), F32),
            pltpu.VMEM((16, CELLS), F32),
        ),
        in_specs=[pl.BlockSpec(memory_space=pltpu.SMEM) if i == 5 else hbm for i in range(12)],
        out_specs=(vmem, vmem, vmem),
        scratch_shapes=[
            tiles(3, 2, 2, 128),
            tiles(3, SLOTS),
            tiles(1, SLOTS),
            tiles(1, SLOTS, dtype=I32),
            tiles(1, SLOTS, dtype=I32),
            tiles(12, HID, dtype=BF16),
            tiles(1, HID),
            tiles(1, HID),
            tiles(6, HID, dtype=BF16),
            tiles(6, 2, 2, 128, dtype=BF16),
            tiles(HID, HID, dtype=BF16),
            tiles(16, HID),
            tiles(16, HID),
            tiles(16, CELLS),
            tiles(4, 8, 128),
            tiles(2, 2, 8, 128),
            tiles(2, 2, 8, 128),
            tiles(16, CELLS),
            tiles(8, 8, 128),
            tiles(8, 8, 128),
            tiles(8, 8, 128),
            tiles(8, 8, 128),
            tiles(64 * CAP, CELLS, dtype=BF16),
            tiles(64 * CAP, 384, dtype=BF16),
            tiles(CELLS, HID),
            tiles(HID, CELLS, dtype=BF16),
            tiles(CELLS, HID, dtype=BF16),
            tiles(CELLS, HID),
            tiles(CELLS, HID, dtype=BF16),
            tiles(CELLS, HID, dtype=BF16),
            tiles(CELLS, HID, dtype=BF16),
            tiles(NBLK, HID // 2, BLK),
            tiles(NBLK, HID // 2, BLK),
            tiles(NBLK, 2, HID // 2, 128),
            tiles(NBLK, 2, 3, 128, 128),
            tiles(NBLK, 2, 128, 128),
            tiles(NBLK, 2, 3, 32, 128),
            tiles(NBLK, 8, 8, 128),
            tiles(NBLK, 7, 8, 128),
            tiles(NBLK, 8, 8, 128),
            tiles(NBLK, 2, 128, 128),
            tiles(32, HID),
            tiles(16, HID),
            tiles(4, 16, 256),
            tiles(3, 16, 256),
            tiles(4, 8, 128),
            tiles(3, 8, 128),
            tiles(8, 8, 128),
            tiles(4, 8, 128),
            tiles(4, 16, 256),
            tiles(4, 16, 256),
            tiles(4, 8, 128),
            tiles(2, 2, 8, 128),
            tiles(2, 2, 8, 128),
            tiles(8, 8, 128),
            tiles(8, 8, 128),
            tiles(8, 8, 128),
            tiles(8, 8, 128),
            pltpu.SemaphoreType.DMA((N_SEMS,)),
            pltpu.SemaphoreType.DMA((N_SEMS,)),
            pltpu.SemaphoreType.DMA((11,)),
        ],
        compiler_params=pltpu.CompilerParams(
            collective_id=0, has_side_effects=True, vmem_limit_bytes=48 << 20
        ),
    )(
        in_hbm(velocity),
        in_hbm(slip),
        in_hbm(rate.reshape(1, SLOTS)),
        in_hbm(owner.T),
        in_hbm(cell.reshape(1, SLOTS)),
        count,
        in_hbm(w_in),
        in_hbm(b_in.reshape(1, HID)),
        in_hbm(w_mid),
        in_hbm(b_mid.reshape(1, HID)),
        in_hbm(w_out.T),
        in_hbm(tau_bar),
    )
    out = [
        jax.ShapeDtypeStruct(s, F32)
        for s in (
            (6, 2, 2, 128),
            (3, 2, 2, 128),
            (3, SLOTS),
            (1, SLOTS),
            (12, HID),
            (1, HID),
            (HID, HID),
            (1, HID),
            (6, HID),
        )
    ]
    stress, vbar, slip_bar, rate_bar, gin, gbin, gmid, gbmid, gout = pl.pallas_call(
        finish,
        name="finish",
        out_shape=out,
        in_specs=[vmem, vmem, vmem],
        out_specs=[hbm if k == 6 else vmem for k in range(9)],
        scratch_shapes=[pltpu.SemaphoreType.DMA((8,))],
        compiler_params=pltpu.CompilerParams(vmem_limit_bytes=4 << 20),
    )(in_vmem(big), in_vmem(sm), in_vmem(po))
    return (
        stress,
        vbar,
        slip_bar,
        rate_bar.reshape(SLOTS),
        gin,
        gbin.reshape(HID),
        gmid,
        gbmid.reshape(HID),
        gout.T,
    )


def solution(mesh):
    return jax.shard_map(
        shards,
        mesh=mesh,
        in_specs=(
            P(None, "gz", "gy", None),
            P(None, ("gz", "gy")),
            P(("gz", "gy")),
            P(("gz", "gy"), None),
            P(("gz", "gy")),
            P(("gz", "gy")),
            P(),
            P(),
            P(),
            P(),
            P(),
            P(None, "gz", "gy", None),
        ),
        out_specs=(
            P(None, "gz", "gy", None),
            P(None, "gz", "gy", None),
            P(None, ("gz", "gy")),
            P(("gz", "gy")),
            P(),
            P(),
            P(),
            P(),
            P(),
        ),
        check_vma=False,
    )
```

```python
import jax
import jax.numpy as jnp
from jax import lax
from jax.experimental import pallas as pl
from jax.experimental.pallas import tpu as pltpu
from jax.sharding import PartitionSpec as P

F32, BF16, I32 = jnp.float32, jnp.bfloat16, jnp.int32
NX_, NZ_, NC_, NY_ = 4, 8, 2, 4
HID, CELLS, SLOTS, CAP = 1024, 512, 512, 16
BLK = 256
NBLK = HID // BLK

(
    G_P1,
    G_P2,
    G_H1,
    G_H2,
    G_RZ,
    G_RX,
    G_SC,
    G_S1,
    G_S2,
    G_S3,
    G_S5,
    G_S6,
    G_S7,
    G_BIG,
) = range(14)
B_RZ, B_GZ, B_FR = (G_BIG + NBLK * i for i in range(3))
B_CORE, B_R1, B_R2, B_G2, B_G1 = (G_BIG + NBLK * (3 + 2 * i) for i in range(5))
N_SEMS = G_BIG + NBLK * 13


def nn(a, b):
    return lax.dot_general(a, b, (((1,), (0,)), ((), ())), preferred_element_type=F32)


def nt(a, b):
    return lax.dot_general(a, b, (((1,), (1,)), ((), ())), preferred_element_type=F32)


def tn(a, b):
    return lax.dot_general(a, b, (((0,), (0,)), ((), ())), preferred_element_type=F32)


def three(value):
    high = value.astype(BF16).astype(F32)
    rest = value - high
    middle = rest.astype(BF16).astype(F32)
    return high, middle, rest - middle


def iota(shape, axis):
    return lax.broadcasted_iota(I32, shape, axis)


def body(
    velocity_in,
    slip_in,
    rate_in,
    owner_in,
    cell_in,
    cnt,
    w_in_in,
    b_in_in,
    w_mid_in,
    b_mid_in,
    w_out_in,
    tau_in,
    out,
    sm_out,
    po,
    velocity,
    slip,
    rate,
    owner,
    cell,
    w_in,
    b_in,
    b_mid,
    w_out,
    tau_bar,
    w_mid,
    w_in16,
    w_out16,
    tau_rows,
    v4,
    hz,
    hy,
    feats,
    m_send,
    r1,
    t1,
    r2,
    onehot,
    fs,
    back2,
    h1,
    h1t,
    ds1,
    h2t,
    g2t,
    g1t,
    cs,
    cb,
    a1,
    b1,
    p2,
    b2,
    p3,
    b3,
    zz,
    y2,
    ssm,
    sc,
    sa,
    sb1,
    spt,
    sb2,
    sz,
    sy,
    sx,
    sxo,
    fb4,
    hz2,
    hy2,
    rts,
    u2,
    t2,
    bk,
    send,
    recv,
    local,
):
    gz, gy = lax.axis_index("gz"), lax.axis_index("gy")
    x, z, c, y = gz // 16, (gz // 2) % 8, gz % 2, gy
    xc = x * 2 + c

    def dev(px, py, pz, pc):
        return {
            "gz": (lax.rem(px, NX_) * NZ_ + lax.rem(pz, NZ_)) * NC_ + lax.rem(pc, NC_),
            "gy": lax.rem(py, NY_),
        }

    def line(gz_, gy_):
        return {"gz": lax.rem(gz_, NX_ * NZ_ * NC_), "gy": lax.rem(gy_, NY_)}

    def start(group, src, dst, where):
        pltpu.make_async_remote_copy(
            src_ref=src,
            dst_ref=dst,
            send_sem=send.at[group],
            recv_sem=recv.at[group],
            device_id=where,
            device_id_type=pl.DeviceIdType.MESH,
        ).start()

    def arrived(group, whole):
        pltpu.make_async_copy(whole, whole, recv.at[group]).wait()

    def left(group, whole):
        pltpu.make_async_copy(whole, whole, send.at[group]).wait()

    sibling = dev(x, y, z, c + 1)
    partners = [dev(x + k // 2, y, z, c + k % 2) for k in range(1, 8)]
    partners += [dev(x, y + k, z, c) for k in range(1, 4)]
    partners += [dev(x, y, z + k, c) for k in range(1, 8)]
    partners += [line(gz + 63 + 2 * c, gy)]
    barrier = pltpu.get_barrier_semaphore()
    for who in partners:
        pl.semaphore_signal(barrier, inc=1, device_id=who, device_id_type=pl.DeviceIdType.MESH)

    loads = [
        pltpu.make_async_copy(src, dst, local.at[i])
        for i, (src, dst) in enumerate(
            (
                (owner_in, owner),
                (cell_in, cell),
                (rate_in, rate),
                (slip_in, slip),
                (velocity_in, velocity),
                (tau_in, tau_bar),
                (w_in_in, w_in),
                (w_out_in, w_out),
                (b_in_in, b_in),
                (b_mid_in, b_mid),
                (w_mid_in, w_mid),
            )
        )
    ]
    for load in loads:
        load.start()

    for load in loads[0:5]:
        load.wait()
    for k in range(4):
        for i in range(3):
            v4[k, i : i + 1, :] = velocity[i, k // 2, k % 2 : k % 2 + 1, :]
    lane = iota((1, SLOTS), 1)
    live = lane < cnt[0]
    slab = owner[...]
    row = (slab >> 4) * 16 + (slab & 1) * 8 + ((slab >> 1) & 7)
    member = jnp.where(iota((64, SLOTS), 0) == row, 1.0, 0.0)
    member16 = member.astype(BF16)
    earlier = jnp.where(iota((SLOTS, SLOTS), 0) < iota((SLOTS, SLOTS), 1), 1.0, 0.0).astype(BF16)
    place = jnp.sum(nn(member16, earlier) * member, axis=0, keepdims=True).astype(I32)
    force = jnp.where(live, rate[...] * slip[...], 0.0)
    four = jnp.concatenate([force, cell[...].astype(F32)], 0)
    sub = iota((128, SLOTS), 0)
    mine = (sub // 4) == place
    wide = jnp.where(mine, jnp.concatenate([four] * 32, 0), 0.0)
    packed = nt(member16, jnp.concatenate(three(wide), 0).astype(BF16))
    packed = packed[:, 0:128] + packed[:, 128:256] + packed[:, 256:384]
    m_send[...] = packed.reshape(8, 8, 128)

    pl.semaphore_wait(barrier, len(partners))

    for k in (5, 4, 7, 3, 6, 2, 1):
        px, pc = lax.rem(x + k // 2, NX_), lax.rem(c + k % 2, NC_)
        start(G_P1, m_send.at[px * 2 + pc], r1.at[xc], dev(px, y, z, pc))

    def halo(group, src, to_z, to_y):
        start(group, src.at[pl.ds(2, 2)], to_z.at[0], line(gz + 1, gy))
        start(group, src.at[pl.ds(0, 2)], to_z.at[1], line(gz + 63, gy))
        start(group, src.at[1], to_y.at[0, 0], line(gz, gy + 1))
        start(group, src.at[3], to_y.at[0, 1], line(gz, gy + 1))
        start(group, src.at[0], to_y.at[1, 0], line(gz, gy + 3))
        start(group, src.at[2], to_y.at[1, 1], line(gz, gy + 3))

    halo(G_H1, v4, hz, hy)

    for load in loads[5:10]:
        load.wait()
    w_in16[...] = jnp.zeros_like(w_in16)
    w_in16[0:12, :] = w_in[...].astype(F32)
    w_out16[...] = jnp.zeros_like(w_out16)
    w_out16[0:6, :] = w_out[...].astype(F32)
    tau_rows[...] = jnp.zeros_like(tau_rows)
    for i in range(6):
        for k in range(2):
            pair = tau_bar[i, k].astype(F32)
            for j in range(2):
                at = 256 * k + 128 * j
                tau_rows[i : i + 1, at : at + 128] = pair[j : j + 1]
    tau = tau_rows[...]
    tau16 = tau.astype(BF16)
    tau_one = jnp.where(iota((16, CELLS), 0) == 6, 1.0, tau).astype(BF16)

    def back_two(q, carry):
        cols = pl.ds(pl.multiple_of(q * BLK, BLK), BLK)
        back2[:, cols] = tn(tau16, w_out16[:, cols].astype(BF16))
        return carry

    lax.fori_loop(0, NBLK, back_two, 0)

    r1[xc] = m_send[xc]
    arrived(G_P1, r1.at[pl.ds(0, 7)])
    for k in range(8):
        t1[k] = r1[:, k, :]
    for k in (4, 3, 5, 2, 6, 1, 7):
        pz = lax.rem(z + k, NZ_)
        start(G_P2, t1.at[pz], r2.at[z], dev(x, y, pz, c))
    r2[z] = t1[z]

    def difference(tiles, from_z, from_y, k):
        kz, ky = k // 2, k % 2
        dz = (tiles[2 + ky] - from_z[0, ky]) if kz == 0 else (from_z[1, ky] - tiles[ky])
        dy = (tiles[2 * kz + 1] - from_y[0, kz]) if ky == 0 else (from_y[1, kz] - tiles[2 * kz])
        return dz * 0.5, dy * 0.5

    def along_x(value):
        return (pltpu.roll(value, 127, 1) - pltpu.roll(value, 1, 1)) * 0.5

    arrived(G_H1, r1)
    feats[...] = jnp.where(iota((16, CELLS), 0) == 12, 1.0, 0.0)
    for k in range(4):
        dz, dy = difference(v4, hz, hy, k)
        for a, d in enumerate((dz, dy, along_x(v4[k]))):
            for i in range(3):
                feats[3 * i + a : 3 * i + a + 1, 128 * k : 128 * k + 128] = d[i : i + 1]

    arrived(G_P2, r2.at[pl.ds(0, 7)])
    got = r2[...].reshape(64, 128)
    cell_of = iota((64, CELLS), 1).astype(F32)
    group_of = iota((64, 128), 1) // 4
    parts = three(got)
    for s in range(CAP):
        rows = slice(64 * s, 64 * s + 64)
        onehot[rows, :] = jnp.where(got[:, 4 * s + 3 : 4 * s + 4] == cell_of, 1.0, 0.0).astype(BF16)
        for j, part in enumerate(parts):
            fs[rows, 128 * j : 128 * j + 128] = jnp.where(group_of == s, part, 0.0).astype(BF16)

    def fold(wide_):
        total = wide_[0:128] + wide_[128:256] + wide_[256:384]
        total = jnp.sum(total.reshape(16, 8, total.shape[1]), axis=0)
        return total[0:3] + total[4:7]

    feats[9:12, :] = fold(tn(fs[...], onehot[...]))
    loads[10].wait()

    feats16 = feats[...].astype(BF16)

    def first(q, carry):
        cols = pl.ds(pl.multiple_of(q * BLK, BLK), BLK)
        pre = tn(feats16, w_in16[:, cols].astype(BF16)) + b_in[:, cols]
        sig = 0.5 * jnp.tanh(0.5 * pre) + 0.5
        hidden = pre * sig
        h1t[:, cols] = hidden.astype(BF16)
        ds1[:, cols] = sig * (1.0 + pre * (1.0 - sig))
        h1[cols, :] = hidden.astype(BF16).T
        return carry

    lax.fori_loop(0, NBLK, first, 0)

    def me1(p):
        return x * (1 - p) + y * p

    def me2(p):
        return y * (1 - p) + x * p

    def peer1(p, k):
        return dev(x + k * (1 - p), y + k * p, z, c)

    def peer2(p, k):
        return dev(x + k * p, y + k * (1 - p), z, c)

    def s1(q):
        for p in range(2):
            arrived(B_CORE + 2 * q + p, cb.at[q, p])
            a1[q, p] = a1[q, p] + cb[q, p]
            for k in (2, 1, 3):
                to = lax.rem(me1(p) + k, 4)
                rows = pl.ds(pl.multiple_of(to * 128, 128), 128)
                start(B_R1 + 2 * q + p, a1.at[q, p, rows], b1.at[q, p, k - 1], peer1(p, k))

    half = HID // 2

    def second(q, carry):
        cols = pl.ds(pl.multiple_of(q * BLK, BLK), BLK)
        pre = nn(h1t[...], w_mid[:, cols]) + b_mid[:, cols]
        sig = 0.5 * jnp.tanh(0.5 * pre) + 0.5
        hidden = (pre * sig).astype(BF16)
        h2t[:, cols] = hidden
        delta = (back2[:, cols] * (sig * (1.0 + pre * (1.0 - sig)))).astype(BF16)
        g2t[:, cols] = delta
        other = nn(h1[pl.ds(pl.multiple_of((1 - c) * half, half), half), :], delta)
        for p in range(2):
            cs[q, p] = other[:, 128 * p : 128 * p + 128]
            start(B_CORE + 2 * q + p, cs.at[q, p], cb.at[q, p], sibling)
        own = nn(h1[pl.ds(pl.multiple_of(c * half, half), half), :], delta)
        a1[q, 0] = own[:, 0:128]
        a1[q, 1] = own[:, 128:256]
        by_hidden, by_delta = nn(tau_one, hidden), nn(tau_one, delta)
        ssm[16:32, cols] = jnp.where(iota((16, BLK), 0) == 6, by_delta, by_hidden)

        @pl.when((q == 1) | (q == 2))
        def _():
            s1(q - 1)

        return carry

    lax.fori_loop(0, NBLK, second, 0)

    def s2(q):
        for p in range(2):
            arrived(B_R1 + 2 * q + p, b1.at[q, p])
            own = a1[q, p, pl.ds(pl.multiple_of(me1(p) * 128, 128), 128), :]
            p2[q, p] = own + b1[q, p, 0] + b1[q, p, 1] + b1[q, p, 2]
            for k in (2, 1, 3):
                rows = pl.ds(pl.multiple_of(lax.rem(me2(p) + k, 4) * 32, 32), 32)
                start(B_R2 + 2 * q + p, p2.at[q, p, rows], b2.at[q, p, k - 1], peer2(p, k))

    def s3(q):
        for p in range(2):
            arrived(B_R2 + 2 * q + p, b2.at[q, p])
            own = p2[q, p, pl.ds(pl.multiple_of(me2(p) * 32, 32), 32), :]
            total = own + b2[q, p, 0] + b2[q, p, 1] + b2[q, p, 2]
            for k in range(8):
                p3[q, k, 4 * p : 4 * p + 4, :] = total[4 * k : 4 * k + 4]
        for k in (4, 3, 5, 2, 6, 1, 7):
            pz = lax.rem(z + k, NZ_)
            start(B_RZ + q, p3.at[q, pz], b3.at[q, k - 1], dev(x, y, pz, c))

    def s4(q):
        arrived(B_RZ + q, b3.at[q])
        zz[q, z] = p3[q, z] + jnp.sum(b3[q], axis=0)
        for k in (4, 3, 5, 2, 6, 1, 7):
            start(B_GZ + q, zz.at[q, z], zz.at[q, z], dev(x, y, z + k, c))

    def s5(q):
        arrived(B_GZ + q, b3.at[q])
        for p in range(2):
            rows = pl.ds(pl.multiple_of(me2(p) * 32, 32), 32)
            y2[q, p, rows, :] = jnp.concatenate([zz[q, k, 4 * p : 4 * p + 4, :] for k in range(8)], 0)
            piece = y2.at[q, p, rows]
            for k in (2, 1, 3):
                start(B_G2 + 2 * q + p, piece, piece, peer2(p, k))

    def s6(q):
        for p in range(2):
            arrived(B_G2 + 2 * q + p, b2.at[q, p])
            rows = pl.ds(pl.multiple_of(c * half + me1(p) * 128, 128), 128)
            cols = slice(BLK * q + 128 * p, BLK * q + 128 * p + 128)
            for k in (2, 1, 3):
                start(B_G1 + 2 * q + p, y2.at[q, p], out.at[rows, cols], peer1(p, k))
            out[rows, cols] = y2[q, p]

    def s7(q):
        for p in range(2):
            arrived(B_G1 + 2 * q + p, b1.at[q, p])
        where = out.at[pl.ds(pl.multiple_of(c * half, half), half), BLK * q : BLK * q + BLK]
        start(B_FR + q, where, where, sibling)

    def s8(q):
        arrived(B_FR + q, cb.at[q])

    def m1():
        arrived(G_SC, sc)
        total = ssm[pl.ds(pl.multiple_of(c * 16, 16), 16), :] + sc[...]
        for k in range(4):
            sa[k] = total[:, 256 * k : 256 * k + 256]
        for k in (2, 1, 3):
            start(G_S1, sa.at[lax.rem(x + k, 4)], sb1.at[k - 1], dev(x + k, y, z, c))

    def m2():
        arrived(G_S1, sb1)
        total = sa[x] + sb1[0] + sb1[1] + sb1[2]
        for k in range(4):
            spt[k] = total[8 * (k // 2) : 8 * (k // 2) + 8, 128 * (k % 2) : 128 * (k % 2) + 128]
        for k in (2, 1, 3):
            start(G_S2, spt.at[lax.rem(y + k, 4)], sb2.at[k - 1], dev(x, y + k, z, c))

    def m3():
        arrived(G_S2, sb2)
        sz[z] = spt[y] + sb2[0] + sb2[1] + sb2[2]
        for k in (4, 3, 5, 2, 6, 1, 7):
            start(G_S3, sz.at[z], sz.at[z], dev(x, y, z + k, c))

    def m5():
        arrived(G_S3, b3.at[0])
        sy[y] = jnp.sum(sz[...], axis=0)
        for k in (2, 1, 3):
            start(G_S5, sy.at[y], sy.at[y], dev(x, y + k, z, c))

    def m6():
        arrived(G_S5, sb2)
        for k in range(4):
            sx[x, 8 * (k // 2) : 8 * (k // 2) + 8, 128 * (k % 2) : 128 * (k % 2) + 128] = sy[k]
        for k in (2, 1, 3):
            start(G_S6, sx.at[x], sx.at[x], dev(x + k, y, z, c))

    def m7():
        arrived(G_S6, sb1)
        start(G_S7, sx, sxo, sibling)

    def m8():
        arrived(G_S7, sc)
        for k in range(4):
            sm_out[pl.ds(pl.multiple_of(c * 16, 16), 16), 256 * k : 256 * k + 256] = sx[k]
            sm_out[pl.ds(pl.multiple_of((1 - c) * 16, 16), 16), 256 * k : 256 * k + 256] = sxo[k]

    def returned():
        arrived(G_RZ, u2.at[pl.ds(0, 7)])
        for k in range(8):
            t2[k] = u2[:, k, :]
        for k in range(1, 8):
            px, pc = lax.rem(x + k // 2, NX_), lax.rem(c + k % 2, NC_)
            start(G_RX, t2.at[px * 2 + pc], bk.at[xc], dev(px, y, z, pc))
        bk[xc] = t2[xc]

    def particles():
        arrived(G_RX, bk.at[pl.ds(0, 7)])
        rows = jnp.concatenate(three(bk[...].reshape(64, 128)), 1).astype(BF16)
        at = tn(rows, member16)
        at = jnp.where(jnp.concatenate([mine] * 3, 0), at, 0.0)
        at = fold(at)
        po[9:12, :] = jnp.where(live, rate[...] * at, 0.0)
        po[12:13, :] = jnp.where(live, jnp.sum(slip[...] * at, axis=0, keepdims=True), 0.0)

    def velocity_bar():
        arrived(G_H2, r1)
        for k in range(4):
            cols = slice(128 * k, 128 * k + 128)
            dz, dy = difference(fb4, hz2, hy2, k)
            dx = along_x(bar[:, cols])
            for i in range(3):
                total = dz[3 * i : 3 * i + 1] + dy[3 * i + 1 : 3 * i + 2] + dx[3 * i + 2 : 3 * i + 3]
                po[6 + i : 7 + i, cols] = -total

    def third(q, carry):
        cols = pl.ds(pl.multiple_of(q * BLK, BLK), BLK)
        delta = (nt(g2t[...], w_mid[cols, :]) * ds1[:, cols]).astype(BF16)
        g1t[:, cols] = delta
        ssm[0:16, cols] = nn(feats16, delta)
        return carry

    lax.fori_loop(0, NBLK, third, 0)
    start(G_SC, ssm.at[pl.ds(pl.multiple_of((1 - c) * 16, 16), 16)], sc, sibling)

    s2(0)
    s1(2)
    bar = nt(w_in16[...].astype(BF16), g1t[...])
    for k in range(4):
        fb4[k] = bar[0:8, 128 * k : 128 * k + 128]
    halo(G_H2, fb4, hz2, hy2)
    s2(1)
    s1(3)
    spread = jnp.concatenate([bar[9:12], jnp.zeros((1, CELLS), F32)], 0)
    spread = jnp.concatenate([spread] * 32, 0)
    picked = nt(onehot[...], jnp.concatenate(three(spread), 0).astype(BF16))
    back = jnp.zeros((64, 128), F32)
    for s in range(CAP):
        block = picked[64 * s : 64 * s + 64]
        block = block[:, 0:128] + block[:, 128:256] + block[:, 256:384]
        back = jnp.where(group_of == s, block, back)
    rts[...] = back.reshape(8, 8, 128)
    for k in range(1, 8):
        pz = lax.rem(z + k, NZ_)
        start(G_RZ, rts.at[pz], u2.at[z], dev(x, y, pz, c))
    u2[z] = rts[z]
    po[0:6, :] = nt(w_out16[...].astype(BF16), h2t[...])[0:6]

    s3(0)
    m1()
    returned()
    s2(2)
    s3(1)
    velocity_bar()
    s2(3)
    s4(0)
    s3(2)
    m2()
    s4(1)
    s3(3)
    particles()
    s5(0)
    m3()
    s4(2)
    s5(1)
    s6(0)
    s4(3)
    s6(1)
    s5(2)
    m5()
    s5(3)
    s6(2)
    m6()
    s6(3)
    s7(0)
    left(G_P1, r1.at[pl.ds(0, 7)])
    left(G_P2, r1.at[pl.ds(0, 7)])
    left(G_H1, r1)
    left(G_H2, r1)
    left(G_RZ, r1.at[pl.ds(0, 7)])
    left(G_RX, r1.at[pl.ds(0, 7)])
    left(G_SC, sc)
    left(G_S1, sb1)
    left(G_S2, sb2)
    left(G_S3, b3.at[0])
    left(G_S5, sb2)
    for q in range(NBLK):
        left(B_RZ + q, b3.at[q])
        left(B_GZ + q, b3.at[q])
        for p in range(2):
            left(B_CORE + 2 * q + p, cb.at[q, p])
            left(B_R1 + 2 * q + p, b1.at[q, p])
            left(B_R2 + 2 * q + p, b2.at[q, p])
            left(B_G2 + 2 * q + p, b2.at[q, p])
    s7(1)
    m7()
    s7(2)
    m8()
    left(G_S6, sb1)
    left(G_S7, sc)
    s7(3)
    for q in range(NBLK):
        for p in range(2):
            left(B_G1 + 2 * q + p, b1.at[q, p])
    for q in range(NBLK):
        s8(q)
        left(B_FR + q, cb.at[q])


def finish(big, sm, po, stress, vbar, slip, rate, gin, gbin, gmid, gbmid, gout, sem):
    copies = [
        pltpu.make_async_copy(big.at[pl.ds(128 * k, 128)], gmid.at[pl.ds(128 * k, 128)], sem.at[k])
        for k in range(8)
    ]
    for copy in copies:
        copy.start()
    for k in range(4):
        cols = slice(128 * k, 128 * k + 128)
        for i in range(6):
            stress[i, k // 2, k % 2 : k % 2 + 1, :] = po[i : i + 1, cols]
        for i in range(3):
            vbar[i, k // 2, k % 2 : k % 2 + 1, :] = po[6 + i : 7 + i, cols]
    slip[...] = po[9:12, :]
    rate[...] = po[12:13, :]
    gin[...] = sm[0:12, :]
    gbin[...] = sm[12:13, :]
    gbmid[...] = sm[22:23, :]
    gout[...] = sm[16:22, :]
    for copy in copies:
        copy.wait()


def tiles(*shape, dtype=F32):
    return pltpu.VMEM(shape, dtype)


def in_hbm(value):
    return pltpu.with_memory_space_constraint(value, pltpu.HBM)


def in_vmem(value):
    return pltpu.with_memory_space_constraint(value, pltpu.VMEM)


def shards(velocity, slip, rate, owner, cell, count, w_in, b_in, w_mid, b_mid, w_out, tau_bar):
    vmem = pl.BlockSpec(memory_space=pltpu.VMEM)
    hbm = pl.BlockSpec(memory_space=pltpu.HBM)
    big, sm, po = pl.pallas_call(
        body,
        name="adjoint",
        out_shape=(
            pltpu.VMEM((HID, HID), F32),
            pltpu.VMEM((32, HID), F32),
            pltpu.VMEM((16, CELLS), F32),
        ),
        in_specs=[pl.BlockSpec(memory_space=pltpu.SMEM) if i == 5 else hbm for i in range(12)],
        out_specs=(vmem, vmem, vmem),
        scratch_shapes=[
            tiles(3, 2, 2, 128),
            tiles(3, SLOTS),
            tiles(1, SLOTS),
            tiles(1, SLOTS, dtype=I32),
            tiles(1, SLOTS, dtype=I32),
            tiles(12, HID, dtype=BF16),
            tiles(1, HID),
            tiles(1, HID),
            tiles(6, HID, dtype=BF16),
            tiles(6, 2, 2, 128, dtype=BF16),
            tiles(HID, HID, dtype=BF16),
            tiles(16, HID),
            tiles(16, HID),
            tiles(16, CELLS),
            tiles(4, 8, 128),
            tiles(2, 2, 8, 128),
            tiles(2, 2, 8, 128),
            tiles(16, CELLS),
            tiles(8, 8, 128),
            tiles(8, 8, 128),
            tiles(8, 8, 128),
            tiles(8, 8, 128),
            tiles(64 * CAP, CELLS, dtype=BF16),
            tiles(64 * CAP, 384, dtype=BF16),
            tiles(CELLS, HID),
            tiles(HID, CELLS, dtype=BF16),
            tiles(CELLS, HID, dtype=BF16),
            tiles(CELLS, HID),
            tiles(CELLS, HID, dtype=BF16),
            tiles(CELLS, HID, dtype=BF16),
            tiles(CELLS, HID, dtype=BF16),
            tiles(NBLK, 2, HID // 2, 128),
            tiles(NBLK, 2, HID // 2, 128),
            tiles(NBLK, 2, HID // 2, 128),
            tiles(NBLK, 2, 3, 128, 128),
            tiles(NBLK, 2, 128, 128),
            tiles(NBLK, 2, 3, 32, 128),
            tiles(NBLK, 8, 8, 128),
            tiles(NBLK, 7, 8, 128),
            tiles(NBLK, 8, 8, 128),
            tiles(NBLK, 2, 128, 128),
            tiles(32, HID),
            tiles(16, HID),
            tiles(4, 16, 256),
            tiles(3, 16, 256),
            tiles(4, 8, 128),
            tiles(3, 8, 128),
            tiles(8, 8, 128),
            tiles(4, 8, 128),
            tiles(4, 16, 256),
            tiles(4, 16, 256),
            tiles(4, 8, 128),
            tiles(2, 2, 8, 128),
            tiles(2, 2, 8, 128),
            tiles(8, 8, 128),
            tiles(8, 8, 128),
            tiles(8, 8, 128),
            tiles(8, 8, 128),
            pltpu.SemaphoreType.DMA((N_SEMS,)),
            pltpu.SemaphoreType.DMA((N_SEMS,)),
            pltpu.SemaphoreType.DMA((11,)),
        ],
        compiler_params=pltpu.CompilerParams(
            collective_id=0, has_side_effects=True, vmem_limit_bytes=48 << 20
        ),
    )(
        in_hbm(velocity),
        in_hbm(slip),
        in_hbm(rate.reshape(1, SLOTS)),
        in_hbm(owner.T),
        in_hbm(cell.reshape(1, SLOTS)),
        count,
        in_hbm(w_in),
        in_hbm(b_in.reshape(1, HID)),
        in_hbm(w_mid),
        in_hbm(b_mid.reshape(1, HID)),
        in_hbm(w_out.T),
        in_hbm(tau_bar),
    )
    out = [
        jax.ShapeDtypeStruct(s, F32)
        for s in (
            (6, 2, 2, 128),
            (3, 2, 2, 128),
            (3, SLOTS),
            (1, SLOTS),
            (12, HID),
            (1, HID),
            (HID, HID),
            (1, HID),
            (6, HID),
        )
    ]
    stress, vbar, slip_bar, rate_bar, gin, gbin, gmid, gbmid, gout = pl.pallas_call(
        finish,
        name="finish",
        out_shape=out,
        in_specs=[vmem, vmem, vmem],
        out_specs=[hbm if k == 6 else vmem for k in range(9)],
        scratch_shapes=[pltpu.SemaphoreType.DMA((8,))],
        compiler_params=pltpu.CompilerParams(vmem_limit_bytes=4 << 20),
    )(in_vmem(big), in_vmem(sm), in_vmem(po))
    return (
        stress,
        vbar,
        slip_bar,
        rate_bar.reshape(SLOTS),
        gin,
        gbin.reshape(HID),
        gmid,
        gbmid.reshape(HID),
        gout.T,
    )


def solution(mesh):
    return jax.shard_map(
        shards,
        mesh=mesh,
        in_specs=(
            P(None, "gz", "gy", None),
            P(None, ("gz", "gy")),
            P(("gz", "gy")),
            P(("gz", "gy"), None),
            P(("gz", "gy")),
            P(("gz", "gy")),
            P(),
            P(),
            P(),
            P(),
            P(),
            P(None, "gz", "gy", None),
        ),
        out_specs=(
            P(None, "gz", "gy", None),
            P(None, "gz", "gy", None),
            P(None, ("gz", "gy")),
            P(("gz", "gy")),
            P(),
            P(),
            P(),
            P(),
            P(),
        ),
        check_vma=False,
    )
```
